256 devices in a mesh: dp: 4 (over y_hi, core), ctx: 64 (over y_lo, z, x).
Axes of the slice: x: 4, y: 4 (y_hi: 2, y_lo: 2; y = y_hi * 2 + y_lo), z: 8, core: 2. Of those that a mesh axis runs over, the one named last changes fastest.
Arguments:
- queries: bfloat16 [4, 4096, 8192], P('dp', None, 'ctx'), may hold values from -6 to 6
- keys_in: bfloat16 [4, 4096, 8192], P('dp', None, 'ctx'), may hold values from -6 to 6
- values_in: bfloat16 [4, 4096, 8192], P('dp', None, 'ctx'), may hold values from -6 to 6
- filters: float32 [256, 128], P(None, 'ctx'), may hold values from -0.6 to 0.6
- grad_out: bfloat16 [4, 4096, 8192], P('dp', None, 'ctx'), may hold values from -6 to 6
Outputs:
- mixed: bfloat16 [4, 4096, 8192], P('dp', None, 'ctx')
- grad_queries: bfloat16 [4, 4096, 8192], P('dp', None, 'ctx')
- grad_keys: bfloat16 [4, 4096, 8192], P('dp', None, 'ctx')
- grad_values: bfloat16 [4, 4096, 8192], P('dp', None, 'ctx')
- grad_filters: float32 [256, 128], P(None, 'ctx')
The draws below stay inside these ranges and needn't reach their ends.
All inputs are finite; a program needn't handle non-finite values.
Results may differ from the reference program's by a relative error of at most 0.0058.
Values may be sent and summed in bfloat16 or wider, within the bound.
A program may use at most 128 MiB of HBM per device.

```python
import math
import jax
import jax.numpy as jnp
from jax import lax

C = 4096
GROUP = 16
FILT = 128
G = 256
L = 8192
BATCH = 4


def draw_filters(key, part):
    key = jax.random.fold_in(key, 7)
    noise_key, rate_key = jax.random.split(key)
    taps_at = jnp.arange(FILT, dtype=jnp.float32)[None, :]
    noise = jax.random.truncated_normal(noise_key, -4.0, 4.0, (G, FILT), jnp.float32)
    decay_len = jnp.exp(jax.random.uniform(rate_key, (G, 1), jnp.float32, math.log(8.0), math.log(400.0)))
    return 0.15 * noise * jnp.exp(-taps_at / decay_len)


def level_of(rng, extent, cuts, smallest, largest):
    level = 1.0
    for dim, blocks in cuts:
        heights = jax.random.uniform(jax.random.fold_in(jax.random.fold_in(rng, 6), dim), (blocks,), jnp.float32, smallest / len(cuts), largest / len(cuts))
        level = level * jnp.repeat(jnp.exp(heights), extent[dim] // blocks).reshape((-1,) + (1,) * (len(extent) - 1 - dim))
    return level


def normal_values(stream_key, extent, spread, most, cuts=(), kind=jnp.bfloat16):
    drawn = spread * jax.random.normal(stream_key, extent, jnp.float32)
    if cuts:
        drawn = drawn * level_of(stream_key, extent, cuts, -0.22, 0.18)
    return jnp.clip(drawn, -most, most).astype(kind)


def setup_inputs(seed: int = 0) -> dict:
    key_of = jax.random.split(jax.random.key(seed), 6)
    return {
        "queries": normal_values(key_of[0], (BATCH, C, L), 1.0, 6.0, ((0, 4), (2, 64))),
        "keys_in": normal_values(key_of[1], (BATCH, C, L), 1.0, 6.0, ((0, 4), (2, 64))),
        "values_in": normal_values(key_of[2], (BATCH, C, L), 1.0, 6.0, ((0, 4), (2, 64))),
        "filters": draw_filters(jax.random.fold_in(key_of[5], 71), 0),
        "grad_out": normal_values(key_of[4], (BATCH, C, L), 1.0, 6.0, ((0, 4), (2, 64))),
    }


def banded(taps):
    width = taps.shape[1]
    padded = jnp.concatenate([taps, jnp.zeros_like(taps)], axis=1)
    rows_at = jnp.arange(width, dtype=jnp.int32)[:, None]
    cols_at = jnp.arange(2 * width, dtype=jnp.int32)[None, :]
    offset = rows_at + width - cols_at
    lag_index = jnp.where((offset >= 0) & (offset < width), offset, width).astype(jnp.int32)
    return jnp.take(padded, lag_index, axis=1)

def apply_filter(signal, taps):
    groups = taps.shape[0]
    block_count = signal.shape[1] // FILT
    shaped = signal.reshape(groups, GROUP, block_count, FILT)
    earlier = jnp.concatenate([jnp.zeros_like(shaped[:, :, :1]), shaped[:, :, :-1]], axis=2)
    matrix = banded(taps)
    own_term = jnp.einsum('gim,gsbm->gsbi', matrix[:, :, FILT:], shaped, precision=lax.Precision.HIGHEST)
    near_term = jnp.einsum('gim,gsbm->gsbi', matrix[:, :, :FILT], earlier, precision=lax.Precision.HIGHEST)
    return (own_term + near_term).reshape(signal.shape)

def reference(queries, keys_in, values_in, filters, grad_out):
    taps_bf = filters.astype(jnp.bfloat16)
    taps_f = lax.optimization_barrier(taps_bf).astype(jnp.float32)

    def one_sequence(items):
        query_s, key_s, value_s, grad_s = items
        query_f = query_s.astype(jnp.float32)
        key_f = key_s.astype(jnp.float32)
        value_f = value_s.astype(jnp.float32)
        grad_f = grad_s.astype(jnp.float32)
        product = (key_f * value_f).astype(jnp.bfloat16)
        product_f = lax.optimization_barrier(product).astype(jnp.float32)
        filtered, pullback = jax.vjp(apply_filter, product_f, taps_f)
        mixed = (query_f * filtered).astype(jnp.bfloat16)
        grad_filtered = (grad_f * query_f).astype(jnp.bfloat16)
        grad_filtered_f = lax.optimization_barrier(grad_filtered).astype(jnp.float32)
        grad_queries = (grad_f * filtered).astype(jnp.bfloat16)
        grad_product, grad_taps = pullback(grad_filtered_f)
        grad_keys = (grad_product * value_f).astype(jnp.bfloat16)
        grad_values = (grad_product * key_f).astype(jnp.bfloat16)
        return (mixed, grad_queries, grad_keys, grad_values, grad_taps)
    mixed, grad_queries, grad_keys, grad_values, grad_taps = lax.map(one_sequence, (queries, keys_in, values_in, grad_out))
    grad_filters = lax.optimization_barrier(jnp.sum(grad_taps.astype(jnp.float32), axis=0))
    return (mixed, grad_queries, grad_keys, grad_values, grad_filters)
```

```python
import jax
import jax.numpy as jnp
import ml_dtypes
import numpy as np
from jax import lax
from jax.experimental import pallas as pl
from jax.experimental.pallas import tpu as pltpu
from jax.sharding import PartitionSpec as P

MESH = pl.DeviceIdType.MESH
BF16 = jnp.bfloat16
F32 = jnp.float32

TAPS = 128
WINDOW = 2 * TAPS
MEMBERS = 16
NX, NZ, NYL, NY = 4, 8, 2, 8
LOADS = 8
STEPS = 16


def split(matrix):
    high = matrix.astype(ml_dtypes.bfloat16)
    low = (matrix - high.astype(np.float64)).astype(ml_dtypes.bfloat16)
    return high, low


def transforms():
    k = np.arange(TAPS, dtype=np.float64)
    n = np.arange(WINDOW, dtype=np.float64)
    angle = 2 * np.pi * np.outer(n, k + 0.5) / WINDOW
    forward = np.concatenate([np.cos(angle), -np.sin(angle)], axis=1)
    inverse = np.concatenate([np.cos(angle), -np.sin(angle)], axis=1).T * (2 / WINDOW)
    fh, fl = split(forward)
    into = np.concatenate([fh[:TAPS], fl[:TAPS], fh[TAPS:], fl[TAPS:]], axis=0)
    ih, il = split(inverse)
    late = np.concatenate([ih[:, TAPS:], il[:, TAPS:]], axis=1)
    early = np.concatenate([ih[:, :TAPS], il[:, :TAPS]], axis=1)
    lag = np.arange(TAPS).reshape(NYL, NZ, NX, 2).transpose(1, 0, 2, 3).reshape(-1)
    th, tl = ih[:, lag].T, il[:, lag].T
    tap = np.concatenate([th, tl, th], axis=1)
    return into, np.stack([late, early]), tap


def dot(a, b):
    return jnp.dot(a, b, preferred_element_type=F32)


def two_parts(a):
    high = a.astype(BF16)
    low = (a - high.astype(F32)).astype(BF16)
    return high, low


def mixer_kernel(
    q_h, k_h, v_h, go_h, f_h, into_h, back_h, tap_h,
    mixed, gq, gk, gv, gfilt,
    q, k, v, go, p, gf, prev, nxt, into, back, tap,
    xg, tg, spec, dspec, sa, ra, sb, rb, sc, rc,
    load_sem, const_sem, hs, hr, xs, xr, zs, zr, ys, yr, as_, ar, bs, br, cs, cr,
):
    rows = q.shape[0]
    lrows, srows = rows // LOADS, rows // STEPS
    per_load = lrows // srows
    groups = srows // MEMBERS
    ctx, dp = lax.axis_index("ctx"), lax.axis_index("dp")
    last = NYL * NZ * NX - 1
    x, z, yl = lax.rem(ctx, NX), lax.rem(lax.div(ctx, NX), NZ), lax.div(ctx, NX * NZ)
    y = lax.div(dp, 2) * 4 + yl * 2 + lax.rem(dp, 2)

    def x_peer(d):
        other = lax.rem(x + d, NX)
        return other, {"ctx": ctx - x + other}

    def z_peer(d):
        other = lax.rem(z + d, NZ)
        return other, {"ctx": ctx + (other - z) * NX}

    def y_peer(d):
        t = lax.rem(y + d, NY)
        its_yl = lax.rem(lax.div(t, 2), 2)
        return its_yl, {
            "dp": lax.div(t, 4) * 2 + lax.rem(t, 2),
            "ctx": ctx + (its_yl - yl) * (NX * NZ),
        }

    right = {"ctx": lax.rem(ctx + 1, last + 1)}
    left = {"ctx": lax.rem(ctx + last, last + 1)}
    other_half = {"ctx": ctx + (1 - 2 * yl) * (NX * NZ)}

    def load(which, i):
        src, dst = ((k_h, k), (v_h, v), (q_h, q), (go_h, go))[which]
        at = pl.ds(pl.multiple_of(i * lrows, lrows), lrows)
        return pltpu.make_async_copy(src.at[at], dst.at[at], load_sem.at[which, i])

    taps_load = pltpu.make_async_copy(f_h, xg.at[x], const_sem.at[0])
    taps_load.start()
    for i in range(LOADS):
        load(0, i).start()
        load(1, i).start()
        load(2, LOADS - 1 - i).start()
        load(3, LOADS - 1 - i).start()
    consts = [
        pltpu.make_async_copy(src, dst, const_sem.at[1 + n])
        for n, (src, dst) in enumerate(((into_h, into), (back_h, back), (tap_h, tap)))
    ]
    for c in consts:
        c.start()

    barrier = pltpu.get_barrier_semaphore()
    greeted = [right, left]
    greeted += [x_peer(d)[1] for d in range(1, NX)]
    greeted += [z_peer(d)[1] for d in range(1, NZ)]
    greeted += [y_peer(d)[1] for d in range(1, NY)]
    for device in greeted:
        pl.semaphore_signal(barrier, inc=1, device_id=device, device_id_type=MESH)

    def at_step(i):
        return pl.ds(pl.multiple_of(i * srows, srows), srows)

    def send_p(i):
        return pltpu.make_async_remote_copy(
            src_ref=p.at[at_step(i)], dst_ref=prev.at[at_step(i)],
            send_sem=hs.at[0, i], recv_sem=hr.at[0, i],
            device_id=right, device_id_type=MESH,
        )

    def send_gf(i):
        return pltpu.make_async_remote_copy(
            src_ref=gf.at[at_step(i)], dst_ref=nxt.at[at_step(i)],
            send_sem=hs.at[1, i], recv_sem=hr.at[1, i],
            device_id=left, device_id_type=MESH,
        )

    def products(i):
        j = LOADS - 1 - i
        load(0, i).wait()
        load(1, i).wait()
        at = pl.ds(pl.multiple_of(i * lrows, lrows), lrows)
        p[at, :] = (k[at, :].astype(F32) * v[at, :].astype(F32)).astype(BF16)
        load(2, j).wait()
        load(3, j).wait()
        at = pl.ds(pl.multiple_of(j * lrows, lrows), lrows)
        gf[at, :] = (q[at, :].astype(F32) * go[at, :].astype(F32)).astype(BF16)

    def send(i):
        for s in range(per_load):
            n = i * per_load + s

            @pl.when(ctx < last)
            def _():
                send_p(n).start()

            @pl.when(ctx > 0)
            def _():
                send_gf(STEPS - 1 - n).start()

    products(0)
    taps_load.wait()
    pl.semaphore_wait(barrier, len(greeted))

    gather_x = [
        pltpu.make_async_remote_copy(
            src_ref=xg.at[x], dst_ref=xg.at[x],
            send_sem=xs.at[d - 1], recv_sem=xr.at[d - 1],
            device_id=x_peer(d)[1], device_id_type=MESH,
        )
        for d in range(1, NX)
    ]
    for c in gather_x:
        c.start()
    send(0)

    @pl.loop(1, LOADS)
    def _(i):
        products(i)
        send(i)

    @pl.when(ctx == 0)
    def _():
        prev[...] = jnp.zeros_like(prev)

    @pl.when(ctx == last)
    def _():
        nxt[...] = jnp.zeros_like(nxt)

    for c in gather_x:
        c.wait()
    mine = jnp.concatenate([xg[i] for i in range(NX)], axis=0)
    tg[yl, z] = mine.astype(BF16).astype(F32)
    gather_z = [
        pltpu.make_async_remote_copy(
            src_ref=tg.at[yl, z], dst_ref=tg.at[yl, z],
            send_sem=zs.at[d - 1], recv_sem=zr.at[d - 1],
            device_id=z_peer(d)[1], device_id_type=MESH,
        )
        for d in range(1, NZ)
    ]
    for c in gather_z:
        c.start()
    for c in gather_z:
        c.wait()
    gather_y = pltpu.make_async_remote_copy(
        src_ref=tg.at[yl], dst_ref=tg.at[yl], send_sem=ys, recv_sem=yr,
        device_id=other_half, device_id_type=MESH,
    )
    gather_y.start()
    for c in consts:
        c.wait()
    gather_y.wait()
    taps = tg[...].reshape(TAPS, -1).T.astype(BF16)
    spec[...] = dot(jnp.concatenate([taps, taps], axis=1), into[:WINDOW, :])

    def spectrum_at(i):
        at = pl.ds(pl.multiple_of(i * groups, groups), groups)

        def spread(a):
            return jnp.broadcast_to(a[:, None, :], (groups, MEMBERS, TAPS)).reshape(srows, TAPS)

        return spread(spec[at, :TAPS]), spread(spec[at, TAPS:])

    def positions(re, im, which):
        high, low = two_parts(jnp.concatenate([re, im], axis=1))
        both = dot(high, back[which])
        return both[:, :TAPS] + both[:, TAPS:] + dot(low, back[which, :, :TAPS])

    def tap_products(i, gre, gim, pre, pim):
        def total(a):
            return jnp.sum(a.reshape(groups, MEMBERS, TAPS), axis=1)

        at = pl.ds(pl.multiple_of(i * groups, groups), groups)
        dspec[at, :TAPS] = total(gre * pre + gim * pim)
        dspec[at, TAPS:] = total(gim * pre - gre * pim)

    def forward_step(i, with_taps):
        @pl.when(ctx > 0)
        def _():
            send_p(i).wait_recv()

        at = at_step(i)
        before, own = prev[at, :], p[at, :]
        window = dot(jnp.concatenate([before, before, own, own], axis=1), into[...])
        re, im = window[:, :TAPS], window[:, TAPS:]
        hre, him = spectrum_at(i)
        filtered = positions(re * hre - im * him, re * him + im * hre, 0)
        mixed[at, :] = (q[at, :].astype(F32) * filtered).astype(BF16)
        gq[at, :] = (go[at, :].astype(F32) * filtered).astype(BF16)
        if with_taps:
            g = gf[at, :]
            gw = dot(jnp.concatenate([g, g], axis=1), into[WINDOW:, :])
            tap_products(i, gw[:, :TAPS], gw[:, TAPS:], re, im)

    def backward_step(i, with_taps):
        @pl.when(ctx < last)
        def _():
            send_gf(i).wait_recv()

        at = at_step(i)
        own, after = gf[at, :], nxt[at, :]
        window = dot(jnp.concatenate([own, own, after, after], axis=1), into[...])
        re, im = window[:, :TAPS], window[:, TAPS:]
        hre, him = spectrum_at(i)
        grad = positions(re * hre + im * him, im * hre - re * him, 1)
        gk[at, :] = (v[at, :].astype(F32) * grad).astype(BF16)
        gv[at, :] = (k[at, :].astype(F32) * grad).astype(BF16)
        if with_taps:
            b = p[at, :]
            pw = dot(jnp.concatenate([b, b], axis=1), into[:WINDOW, :])
            tap_products(i, re, im, pw[:, :TAPS], pw[:, TAPS:])

    def steps(start, stop, with_taps):
        @pl.loop(start, stop)
        def _(i):
            forward_step(i, with_taps)
            backward_step(STEPS - 1 - i, with_taps)

    steps(0, STEPS // 2, True)

    high, low = two_parts(dspec[...])
    grads = lax.dot_general(
        tap[...], jnp.concatenate([high, high, low], axis=1),
        (((1,), (1,)), ((), ())), preferred_element_type=F32,
    )
    sa[...] = grads.reshape(sa.shape)
    ra[z] = sa[z]
    reduce_z = []
    for d in range(1, NZ):
        other, device = z_peer(d)
        reduce_z.append(
            pltpu.make_async_remote_copy(
                src_ref=sa.at[other], dst_ref=ra.at[z],
                send_sem=as_.at[d - 1], recv_sem=ar.at[d - 1],
                device_id=device, device_id_type=MESH,
            )
        )
    for c in reduce_z:
        c.start()

    steps(STEPS // 2, 11, False)

    for c in reduce_z:
        c.wait()
    sb[...] = jnp.sum(ra[...], axis=0).reshape(sb.shape)
    rb[y] = sb[yl]
    reduce_y = []
    for d in range(1, NY):
        its_yl, device = y_peer(d)
        reduce_y.append(
            pltpu.make_async_remote_copy(
                src_ref=sb.at[its_yl], dst_ref=rb.at[y],
                send_sem=bs.at[d - 1], recv_sem=br.at[d - 1],
                device_id=device, device_id_type=MESH,
            )
        )
    for c in reduce_y:
        c.start()

    steps(11, 13, False)

    for c in reduce_y:
        c.wait()
    part = jnp.sum(rb[...], axis=0)
    for i in range(NX):
        sc[i] = part[2 * i : 2 * i + 2]
    rc[x] = sc[x]
    reduce_x = []
    for d in range(1, NX):
        other, device = x_peer(d)
        reduce_x.append(
            pltpu.make_async_remote_copy(
                src_ref=sc.at[other], dst_ref=rc.at[x],
                send_sem=cs.at[d - 1], recv_sem=cr.at[d - 1],
                device_id=device, device_id_type=MESH,
            )
        )
    for c in reduce_x:
        c.start()

    steps(13, STEPS, False)

    for c in reduce_x:
        c.wait()
    gfilt[...] = jnp.sum(rc[...], axis=0)

    @pl.loop(0, STEPS)
    def _(i):
        @pl.when(ctx < last)
        def _():
            send_p(i).wait_send()

        @pl.when(ctx > 0)
        def _():
            send_gf(i).wait_send()


def write_kernel(*refs):
    count = len(refs) // 2
    sems = refs[-1]
    copies = [
        pltpu.make_async_copy(refs[i], refs[count + i], sems.at[i]) for i in range(count)
    ]
    for c in copies:
        c.start()
    for c in copies:
        c.wait()


def local(queries, keys_in, values_in, filters, grad_out):
    rows, width = queries.shape[1:]
    groups = filters.shape[0]
    into, back, tap = (jnp.asarray(m) for m in transforms())
    slab = (rows, width)
    dma = pltpu.SemaphoreType.DMA
    anywhere = pl.BlockSpec(memory_space=pl.ANY)
    in_vmem = pl.BlockSpec(memory_space=pltpu.VMEM)
    operands = [queries[0], keys_in[0], values_in[0], grad_out[0], filters.T, into, back, tap]
    operands = [pltpu.with_memory_space_constraint(a, pltpu.HBM) for a in operands]
    outs = pl.pallas_call(
        mixer_kernel,
        out_shape=[pltpu.VMEM(slab, BF16)] * 4 + [pltpu.VMEM((2, groups), F32)],
        in_specs=[anywhere] * len(operands),
        out_specs=[in_vmem] * 5,
        scratch_shapes=[
            *[pltpu.VMEM(slab, BF16)] * 8,
            pltpu.VMEM(into.shape, BF16), pltpu.VMEM(back.shape, BF16), pltpu.VMEM(tap.shape, BF16),
            pltpu.VMEM((NX, 2, groups), F32), pltpu.VMEM((NYL, NZ, 2 * NX, groups), F32),
            pltpu.VMEM((groups, WINDOW), F32), pltpu.VMEM((groups, WINDOW), F32),
            pltpu.VMEM((NZ, 16, groups), F32), pltpu.VMEM((NZ, 16, groups), F32),
            pltpu.VMEM((NYL, 8, groups), F32), pltpu.VMEM((NY, 8, groups), F32),
            pltpu.VMEM((NX, 2, groups), F32), pltpu.VMEM((NX, 2, groups), F32),
            dma((4, LOADS)), dma((4,)), dma((2, STEPS)), dma((2, STEPS)),
            dma((NX - 1,)), dma((NX - 1,)), dma((NZ - 1,)), dma((NZ - 1,)), dma, dma,
            dma((NZ - 1,)), dma((NZ - 1,)), dma((NY - 1,)), dma((NY - 1,)),
            dma((NX - 1,)), dma((NX - 1,)),
        ],
        compiler_params=pltpu.CompilerParams(
            collective_id=0, has_side_effects=True, vmem_limit_bytes=40 * 2**20
        ),
        name="mixer",
    )(*operands)
    outs = [pltpu.with_memory_space_constraint(a, pltpu.VMEM) for a in outs]
    written = pl.pallas_call(
        write_kernel,
        out_shape=[pltpu.HBM(a.shape, a.dtype) for a in outs],
        in_specs=[anywhere] * 5,
        out_specs=[anywhere] * 5,
        scratch_shapes=[dma((5,))],
        compiler_params=pltpu.CompilerParams(vmem_limit_bytes=2**20),
        name="write",
    )(*outs)
    return (*[a[None] for a in written[:4]], written[4].T)


def solution(mesh):
    return jax.shard_map(
        local,
        mesh=mesh,
        in_specs=(
            P("dp", None, "ctx"),
            P("dp", None, "ctx"),
            P("dp", None, "ctx"),
            P(None, "ctx"),
            P("dp", None, "ctx"),
        ),
        out_specs=(
            P("dp", None, "ctx"),
            P("dp", None, "ctx"),
            P("dp", None, "ctx"),
            P("dp", None, "ctx"),
            P(None, "ctx"),
        ),
        check_vma=False,
    )
```

```python
import jax
import jax.numpy as jnp
import ml_dtypes
import numpy as np
from jax import lax
from jax.experimental import pallas as pl
from jax.experimental.pallas import tpu as pltpu
from jax.sharding import PartitionSpec as P

MESH = pl.DeviceIdType.MESH
BF16 = jnp.bfloat16
F32 = jnp.float32

TAPS = 128
WINDOW = 2 * TAPS
MEMBERS = 16
NX, NZ, NYL, NY = 4, 8, 2, 8
LOADS = 8
STEPS = 16
AHEAD, LATER, DEEP = 8, 2, 4


def split(matrix):
    high = matrix.astype(ml_dtypes.bfloat16)
    low = (matrix - high.astype(np.float64)).astype(ml_dtypes.bfloat16)
    return high, low


def transforms():
    k = np.arange(TAPS, dtype=np.float64)
    n = np.arange(WINDOW, dtype=np.float64)
    angle = 2 * np.pi * np.outer(n, k + 0.5) / WINDOW
    forward = np.concatenate([np.cos(angle), -np.sin(angle)], axis=1)
    inverse = np.concatenate([np.cos(angle), -np.sin(angle)], axis=1).T * (2 / WINDOW)
    fh, fl = split(forward)
    into = np.concatenate([fh[:TAPS], fl[:TAPS], fh[TAPS:], fl[TAPS:]], axis=0)
    ih, il = split(inverse)
    late = np.concatenate([ih[:, TAPS:], il[:, TAPS:]], axis=1)
    early = np.concatenate([ih[:, :TAPS], il[:, :TAPS]], axis=1)
    lag = np.arange(TAPS).reshape(NYL, NZ, NX, 2).transpose(1, 0, 2, 3).reshape(-1)
    th, tl = ih[:, lag].T, il[:, lag].T
    tap = np.concatenate([th, tl, th], axis=1)
    return into, np.stack([late, early]), tap


def dot(a, b):
    return jnp.dot(a, b, preferred_element_type=F32)


def two_parts(a):
    high = a.astype(BF16)
    low = (a - high.astype(F32)).astype(BF16)
    return high, low


def mixer_kernel(
    q_h, k_h, v_h, go_h, f_h, into_h, back_h, tap_h,
    mixed, gq, gk, gv, gfilt,
    q, k, v, go, p, gf, prev, nxt, into, back, tap,
    xg, zg, spec, dspec, fspec, bspec, sa, ra, sb, rb, sc, rc,
    load_sem, const_sem, hs, hr, xs, xr, zs, zr, ys, yr, as_, ar, bs, br, cs, cr,
):
    rows = q.shape[0]
    lrows, srows = rows // LOADS, rows // STEPS
    per_load = lrows // srows
    groups = srows // MEMBERS
    ctx, dp = lax.axis_index("ctx"), lax.axis_index("dp")
    last = NYL * NZ * NX - 1
    x, z, yl = lax.rem(ctx, NX), lax.rem(lax.div(ctx, NX), NZ), lax.div(ctx, NX * NZ)
    y = lax.div(dp, 2) * 4 + yl * 2 + lax.rem(dp, 2)

    def x_peer(d):
        other = lax.rem(x + d, NX)
        return other, {"ctx": ctx - x + other}

    def z_peer(d):
        other = lax.rem(z + d, NZ)
        return other, {"ctx": ctx + (other - z) * NX}

    def beside_peer(d):
        other = lax.rem(z + d, NZ)
        return {"ctx": ctx + (other - z) * NX + 1 - 2 * lax.rem(x, 2)}

    right = {"ctx": lax.rem(ctx + 1, last + 1)}
    left = {"ctx": lax.rem(ctx + last, last + 1)}
    half = NX * NZ
    other_half = {"ctx": ctx + (1 - 2 * yl) * half}
    unable = (ctx == 0) | (ctx == last)
    from_low, to_low = half - NX, half + NX - 1
    helper = (ctx == from_low) | (ctx == to_low)
    helped = (ctx == half) | (ctx == half - 1)
    helper_pair = {"ctx": jnp.where(ctx == from_low, half, jnp.where(ctx == half, from_low, jnp.where(ctx == to_low, half - 1, to_low)))}
    aside = 1 - 2 * lax.div(x, 2)

    def turn_z(amount):
        return lax.rem(z + amount + NZ, NZ)

    def sum_y_peer(t, amount):
        its_yl = (t // 2) % 2
        return its_yl, {
            "dp": (t // 4) * 2 + t % 2,
            "ctx": ctx + (its_yl - yl) * half + (turn_z(amount) - z) * NX,
        }

    def sum_x_peer(t, amount):
        return {"ctx": ctx + t - x + (turn_z(amount) - z) * NX}

    def load(which, i):
        src, dst = ((k_h, k), (v_h, v), (q_h, q), (go_h, go))[which]
        at = pl.ds(pl.multiple_of(i * lrows, lrows), lrows)
        return pltpu.make_async_copy(src.at[at], dst.at[at], load_sem.at[which, i])

    taps_load = pltpu.make_async_copy(f_h, xg.at[x], const_sem.at[0])
    taps_load.start()
    for i in range(LOADS):
        load(0, i).start()
        load(1, i).start()
        load(2, LOADS - 1 - i).start()
        load(3, LOADS - 1 - i).start()
    consts = [
        pltpu.make_async_copy(src, dst, const_sem.at[1 + n])
        for n, (src, dst) in enumerate(((into_h, into), (back_h, back), (tap_h, tap)))
    ]
    for c in consts:
        c.start()

    barrier = pltpu.get_barrier_semaphore()
    middle = (x == 1) | (x == 2)
    greeted = [right, left]
    greeted += [x_peer(d)[1] for d in range(1, NX)]
    greeted += [z_peer(d)[1] for d in range(1, NZ)]
    greeted += [sum_y_peer(t, -aside)[1] for t in range(NY)]
    greeted += [sum_x_peer(t, 2 * (t // 2) - 1) for t in range(NX)]
    for device in greeted:
        pl.semaphore_signal(barrier, inc=1, device_id=device, device_id_type=MESH)

    @pl.when(jnp.logical_not(middle))
    def _():
        for d in range(1, NZ):
            pl.semaphore_signal(barrier, inc=1, device_id=beside_peer(d), device_id_type=MESH)

    @pl.when(jnp.logical_not(helped))
    def _():
        pl.semaphore_signal(barrier, inc=1, device_id=other_half, device_id_type=MESH)

    @pl.when(helped)
    def _():
        pl.semaphore_signal(barrier, inc=1, device_id=helper_pair, device_id_type=MESH)

    def at_step(i):
        return pl.ds(pl.multiple_of(i * srows, srows), srows)

    def send_p(i):
        return pltpu.make_async_remote_copy(
            src_ref=p.at[at_step(i)], dst_ref=prev.at[at_step(i)],
            send_sem=hs.at[0, i], recv_sem=hr.at[0, i],
            device_id=right, device_id_type=MESH,
        )

    def send_gf(i):
        return pltpu.make_async_remote_copy(
            src_ref=gf.at[at_step(i)], dst_ref=nxt.at[at_step(i)],
            send_sem=hs.at[1, i], recv_sem=hr.at[1, i],
            device_id=left, device_id_type=MESH,
        )

    def products(i):
        j = LOADS - 1 - i
        load(0, i).wait()
        load(1, i).wait()
        at = pl.ds(pl.multiple_of(i * lrows, lrows), lrows)
        p[at, :] = (k[at, :].astype(F32) * v[at, :].astype(F32)).astype(BF16)
        load(2, j).wait()
        load(3, j).wait()
        at = pl.ds(pl.multiple_of(j * lrows, lrows), lrows)
        gf[at, :] = (q[at, :].astype(F32) * go[at, :].astype(F32)).astype(BF16)

    products(0)
    taps_load.wait()
    count = len(greeted) + jnp.where(middle, NZ - 1, 0) + jnp.where(unable, 0, 1) + jnp.where(helper, 1, 0)
    pl.semaphore_wait(barrier, count)

    gather_x = [
        pltpu.make_async_remote_copy(
            src_ref=xg.at[x], dst_ref=xg.at[x],
            send_sem=xs.at[d - 1], recv_sem=xr.at[d - 1],
            device_id=x_peer(d)[1], device_id_type=MESH,
        )
        for d in range(1, NX)
    ]
    gather_z = [
        [
            pltpu.make_async_remote_copy(
                src_ref=zg.at[yl, z], dst_ref=zg.at[yl, z],
                send_sem=zs.at[n, d - 1], recv_sem=zr.at[d - 1],
                device_id=device, device_id_type=MESH,
            )
            for n, device in enumerate((z_peer(d)[1], beside_peer(d)))
        ]
        for d in range(1, NZ)
    ]
    gather_y, gather_help = (
        pltpu.make_async_remote_copy(
            src_ref=zg.at[yl], dst_ref=zg.at[yl], send_sem=ys.at[n], recv_sem=yr,
            device_id=device, device_id_type=MESH,
        )
        for n, device in enumerate((other_half, helper_pair))
    )
    reduce_z, reduce_y, reduce_x = [], [], []
    for d in range(1, NZ):
        other, device = z_peer(d)
        reduce_z.append(
            pltpu.make_async_remote_copy(
                src_ref=sa.at[lax.rem(other + 2 * aside + NZ, NZ)], dst_ref=ra.at[z],
                send_sem=as_.at[d - 1], recv_sem=ar.at[d - 1],
                device_id=device, device_id_type=MESH,
            )
        )
    for t in range(NY):
        its_yl, device = sum_y_peer(t, aside)
        reduce_y.append(
            pltpu.make_async_remote_copy(
                src_ref=sb.at[its_yl], dst_ref=rb.at[y],
                send_sem=bs.at[t], recv_sem=br.at[y],
                device_id=device, device_id_type=MESH,
            )
        )
    for t in range(NX):
        reduce_x.append(
            pltpu.make_async_remote_copy(
                src_ref=sc.at[t], dst_ref=rc.at[x],
                send_sem=cs.at[t], recv_sem=cr.at[x],
                device_id=sum_x_peer(t, aside), device_id_type=MESH,
            )
        )

    def wait_sum(copies, landed, recv_sems):
        for n, c in enumerate(copies):
            c.wait_send()
            pltpu.make_async_remote_copy(
                src_ref=landed.at[n], dst_ref=landed.at[n],
                send_sem=recv_sems.at[n], recv_sem=recv_sems.at[n],
                device_id=right, device_id_type=MESH,
            ).wait_recv()

    for c in gather_x:
        c.start()

    def send(n):
        @pl.when(ctx < last)
        def _():
            send_p(n).start()

        @pl.when(ctx > 0)
        def _():
            send_gf(STEPS - 1 - n).start()

    for s in range(per_load):
        send(s)

    @pl.loop(1, LOADS)
    def _(i):
        products(i)

        @pl.when(i * per_load < AHEAD)
        def _():
            for s in range(per_load):
                send(i * per_load + s)

    @pl.when(ctx == 0)
    def _():
        prev[...] = jnp.zeros_like(prev)

    @pl.when(ctx == last)
    def _():
        nxt[...] = jnp.zeros_like(nxt)

    for c in consts:
        c.wait()
    for c in gather_x:
        c.wait()
    mine = jnp.concatenate([xg[i] for i in range(NX)], axis=0)
    zg[yl, z] = jnp.concatenate([mine[:, :TAPS], mine[:, TAPS:]], axis=0).astype(BF16)

    @pl.when(middle)
    def _():
        for pair in gather_z:
            for c in pair:
                c.start()

    def spread(a):
        return jnp.broadcast_to(a[:, None, :], (groups, MEMBERS, TAPS)).reshape(srows, TAPS)

    def group_rows(i):
        return pl.ds(pl.multiple_of(i * groups, groups), groups)

    def positions(re, im, which):
        high, low = two_parts(jnp.concatenate([re, im], axis=1))
        both = dot(high, back[which])
        return both[:, :TAPS] + both[:, TAPS:] + dot(low, back[which, :, :TAPS])

    def arrived(i):
        @pl.when(ctx > 0)
        def _():
            send_p(i).wait_recv()

        @pl.when(ctx < last)
        def _():
            send_gf(STEPS - 1 - i).wait_recv()

    def forward_window(i):
        before, own = prev[at_step(i), :], p[at_step(i), :]
        return dot(jnp.concatenate([before, before, own, own], axis=1), into[...])

    def backward_window(i):
        own, after = gf[at_step(i), :], nxt[at_step(i), :]
        return dot(jnp.concatenate([own, own, after, after], axis=1), into[...])

    def forward_outputs(i, window):
        at = at_step(i)
        re, im = window[:, :TAPS], window[:, TAPS:]
        hre, him = spread(spec[group_rows(i), :TAPS]), spread(spec[group_rows(i), TAPS:])
        filtered = positions(re * hre - im * him, re * him + im * hre, 0)
        mixed[at, :] = (q[at, :].astype(F32) * filtered).astype(BF16)
        gq[at, :] = (go[at, :].astype(F32) * filtered).astype(BF16)

    def backward_outputs(i, window):
        at = at_step(i)
        re, im = window[:, :TAPS], window[:, TAPS:]
        hre, him = spread(spec[group_rows(i), :TAPS]), spread(spec[group_rows(i), TAPS:])
        grad = positions(re * hre + im * him, im * hre - re * him, 1)
        gk[at, :] = (v[at, :].astype(F32) * grad).astype(BF16)
        gv[at, :] = (k[at, :].astype(F32) * grad).astype(BF16)

    def tap_products(i, g, b):
        def total(a):
            return jnp.sum(a.reshape(groups, MEMBERS, TAPS), axis=1)

        gre, gim, bre, bim = g[:, :TAPS], g[:, TAPS:], b[:, :TAPS], b[:, TAPS:]
        dspec[group_rows(i), :TAPS] = total(gre * bre + gim * bim)
        dspec[group_rows(i), TAPS:] = total(gim * bre - gre * bim)

    @pl.loop(0, STEPS // 2)
    def _(i):
        @pl.when(i + AHEAD < STEPS // 2 + LATER)
        def _():
            send(i + AHEAD)

        arrived(i)
        j = STEPS - 1 - i
        fw, bw = forward_window(i), backward_window(j)
        g, b = gf[at_step(i), :], p[at_step(j), :]
        gw = dot(jnp.concatenate([g, g], axis=1), into[WINDOW:, :])
        bp = dot(jnp.concatenate([b, b], axis=1), into[:WINDOW, :])
        tap_products(i, gw, fw)
        tap_products(j, bw, bp)
        fspec[at_step(i), :] = fw
        bspec[at_step(i), :] = bw

        @pl.when(i == 2)
        def _():
            for pair in gather_z:
                pair[0].wait_recv()

            @pl.when(jnp.logical_not(unable))
            def _():
                gather_y.start()

            @pl.when(helper)
            def _():
                gather_help.start()

    high, low = two_parts(dspec[...])
    grads = lax.dot_general(
        tap[...], jnp.concatenate([high, high, low], axis=1),
        (((1,), (1,)), ((), ())), preferred_element_type=F32,
    )
    sa[...] = grads.reshape(sa.shape)
    ra[z] = sa[turn_z(2 * aside)]
    for c in reduce_z:
        c.start()
    for n in range(LATER, DEEP):
        send(STEPS // 2 + n)

    gather_y.wait_recv()

    @pl.when(jnp.logical_not(unable))
    def _():
        gather_y.wait_send()

    @pl.when(helper)
    def _():
        gather_help.wait_send()

    @pl.when(middle)
    def _():
        for pair in gather_z:
            for c in pair:
                c.wait_send()

    tiles = [zg[a, b].astype(F32) for a in range(NYL) for b in range(NZ)]
    taps = jnp.concatenate([jnp.concatenate([t[:8], t[8:]], axis=1) for t in tiles], axis=0).T.astype(BF16)
    spec[...] = dot(jnp.concatenate([taps, taps], axis=1), into[:WINDOW, :])

    @pl.loop(STEPS // 2, STEPS)
    def _(i):
        @pl.when(i + DEEP < STEPS)
        def _():
            send(i + DEEP)

        old = i - STEPS // 2
        forward_outputs(old, fspec[at_step(old), :])
        backward_outputs(STEPS - 1 - old, bspec[at_step(old), :])
        arrived(i)
        forward_outputs(i, forward_window(i))
        backward_outputs(STEPS - 1 - i, backward_window(STEPS - 1 - i))

        @pl.when(i == STEPS // 2 + 1)
        def _():
            for c in reduce_z:
                c.wait()
            sb[...] = jnp.sum(ra[...], axis=0).reshape(sb.shape)
            for c in reduce_y:
                c.start()

        @pl.when(i == STEPS // 2 + 4)
        def _():
            wait_sum(reduce_y, rb, br)
            part = jnp.sum(rb[...], axis=0)
            for n in range(NX):
                sc[n] = part[2 * n : 2 * n + 2]
            for c in reduce_x:
                c.start()

    wait_sum(reduce_x, rc, cr)
    gfilt[...] = jnp.sum(rc[...], axis=0)

    @pl.loop(0, STEPS)
    def _(i):
        @pl.when(ctx < last)
        def _():
            send_p(i).wait_send()

        @pl.when(ctx > 0)
        def _():
            send_gf(i).wait_send()


def write_kernel(*refs):
    count = len(refs) // 2
    sems = refs[-1]
    copies = [
        pltpu.make_async_copy(refs[i], refs[count + i], sems.at[i]) for i in range(count)
    ]
    for c in copies:
        c.start()
    for c in copies:
        c.wait()


def local(queries, keys_in, values_in, filters, grad_out):
    rows, width = queries.shape[1:]
    groups = filters.shape[0]
    into, back, tap = (jnp.asarray(m) for m in transforms())
    slab = (rows, width)
    dma = pltpu.SemaphoreType.DMA
    anywhere = pl.BlockSpec(memory_space=pl.ANY)
    in_vmem = pl.BlockSpec(memory_space=pltpu.VMEM)
    operands = [queries[0], keys_in[0], values_in[0], grad_out[0], filters.T, into, back, tap]
    operands = [pltpu.with_memory_space_constraint(a, pltpu.HBM) for a in operands]
    outs = pl.pallas_call(
        mixer_kernel,
        out_shape=[pltpu.VMEM(slab, BF16)] * 4 + [pltpu.VMEM((2, groups), F32)],
        in_specs=[anywhere] * len(operands),
        out_specs=[in_vmem] * 5,
        scratch_shapes=[
            *[pltpu.VMEM(slab, BF16)] * 8,
            pltpu.VMEM(into.shape, BF16), pltpu.VMEM(back.shape, BF16), pltpu.VMEM(tap.shape, BF16),
            pltpu.VMEM((NX, 2, groups), F32), pltpu.VMEM((NYL, NZ, 16, TAPS), BF16),
            pltpu.VMEM((groups, WINDOW), F32), pltpu.VMEM((groups, WINDOW), F32),
            pltpu.VMEM((rows // 2, WINDOW), F32), pltpu.VMEM((rows // 2, WINDOW), F32),
            pltpu.VMEM((NZ, 16, groups), F32), pltpu.VMEM((NZ, 16, groups), F32),
            pltpu.VMEM((NYL, 8, groups), F32), pltpu.VMEM((NY, 8, groups), F32),
            pltpu.VMEM((NX, 2, groups), F32), pltpu.VMEM((NX, 2, groups), F32),
            dma((4, LOADS)), dma((4,)), dma((2, STEPS)), dma((2, STEPS)),
            dma((NX - 1,)), dma((NX - 1,)), dma((2, NZ - 1)), dma((NZ - 1,)), dma((2,)), dma,
            dma((NZ - 1,)), dma((NZ - 1,)), dma((NY,)), dma((NY,)),
            dma((NX,)), dma((NX,)),
        ],
        compiler_params=pltpu.CompilerParams(
            collective_id=0, has_side_effects=True, vmem_limit_bytes=40 * 2**20
        ),
        name="mixer",
    )(*operands)
    outs = [pltpu.with_memory_space_constraint(a, pltpu.VMEM) for a in outs]
    written = pl.pallas_call(
        write_kernel,
        out_shape=[pltpu.HBM(a.shape, a.dtype) for a in outs],
        in_specs=[anywhere] * 5,
        out_specs=[anywhere] * 5,
        scratch_shapes=[dma((5,))],
        compiler_params=pltpu.CompilerParams(vmem_limit_bytes=2**20),
        name="write",
    )(*outs)
    return (*[a[None] for a in written[:4]], written[4].T)


def solution(mesh):
    return jax.shard_map(
        local,
        mesh=mesh,
        in_specs=(
            P("dp", None, "ctx"),
            P("dp", None, "ctx"),
            P("dp", None, "ctx"),
            P(None, "ctx"),
            P("dp", None, "ctx"),
        ),
        out_specs=(
            P("dp", None, "ctx"),
            P("dp", None, "ctx"),
            P("dp", None, "ctx"),
            P("dp", None, "ctx"),
            P(None, "ctx"),
        ),
        check_vma=False,
    )
```

```python
import jax
import jax.numpy as jnp
import ml_dtypes
import numpy as np
from jax import lax
from jax.experimental import pallas as pl
from jax.experimental.pallas import tpu as pltpu
from jax.sharding import PartitionSpec as P

MESH = pl.DeviceIdType.MESH
BF16 = jnp.bfloat16
F32 = jnp.float32

TAPS = 128
WINDOW = 2 * TAPS
MEMBERS = 16
NX, NZ, NYL, NY = 4, 8, 2, 8
LOADS = 8
STEPS = 16
AHEAD, LATER, DEEP = 8, 2, 4


def split(matrix):
    high = matrix.astype(ml_dtypes.bfloat16)
    low = (matrix - high.astype(np.float64)).astype(ml_dtypes.bfloat16)
    return high, low


def transforms():
    k = np.arange(TAPS, dtype=np.float64)
    n = np.arange(WINDOW, dtype=np.float64)
    angle = 2 * np.pi * np.outer(n, k + 0.5) / WINDOW
    forward = np.concatenate([np.cos(angle), -np.sin(angle)], axis=1)
    inverse = np.concatenate([np.cos(angle), -np.sin(angle)], axis=1).T * (2 / WINDOW)
    fh, fl = split(forward)
    into = np.concatenate([fh[:TAPS], fl[:TAPS], fh[TAPS:], fl[TAPS:]], axis=0)
    ih, il = split(inverse)
    late = np.concatenate([ih[:, TAPS:], il[:, TAPS:]], axis=1)
    early = np.concatenate([ih[:, :TAPS], il[:, :TAPS]], axis=1)
    lag = np.arange(TAPS).reshape(NYL, NZ, NX, 2).transpose(1, 0, 2, 3).reshape(-1)
    th, tl = ih[:, lag].T, il[:, lag].T
    tap = np.concatenate([th, tl, th], axis=1)
    return into, np.stack([late, early]), tap


def dot(a, b):
    return jnp.dot(a, b, preferred_element_type=F32)


def two_parts(a):
    high = a.astype(BF16)
    low = (a - high.astype(F32)).astype(BF16)
    return high, low


def wrap(value, size):
    return value - jnp.where(value >= size, size, 0)


def mixer_kernel(
    q_h, k_h, v_h, go_h, f_h, into_h, back_h, tap_h,
    mixed, gq, gk, gv, gfilt,
    q, k, v, go, p, gf, prev, nxt, into, back, tap,
    xg, zg, spec, dspec, fspec, bspec, sa, ra, sb, rb, sc, rc,
    load_sem, const_sem, hs, hr, xs, xr, zs, zr, ys, yr, as_, ar, bs, br, cs, cr,
):
    rows = q.shape[0]
    lrows, srows = rows // LOADS, rows // STEPS
    per_load = lrows // srows
    groups = srows // MEMBERS
    ctx, dp = lax.axis_index("ctx"), lax.axis_index("dp")
    last = NYL * NZ * NX - 1
    x, z, yl = lax.rem(ctx, NX), lax.rem(lax.div(ctx, NX), NZ), lax.div(ctx, NX * NZ)
    y = lax.div(dp, 2) * 4 + yl * 2 + lax.rem(dp, 2)

    def x_peer(d):
        other = wrap(x + d, NX)
        return other, {"ctx": ctx - x + other}

    def z_peer(d):
        other = wrap(z + d, NZ)
        return other, {"ctx": ctx + (other - z) * NX}

    def beside_peer(d):
        other = wrap(z + d, NZ)
        return {"ctx": ctx + (other - z) * NX + 1 - 2 * lax.rem(x, 2)}

    right = {"ctx": wrap(ctx + 1, last + 1)}
    left = {"ctx": wrap(ctx + last, last + 1)}
    half = NX * NZ
    other_half = {"ctx": ctx + (1 - 2 * yl) * half}
    unable = (ctx == 0) | (ctx == last)
    from_low, to_low = half - NX, half + NX - 1
    helper = (ctx == from_low) | (ctx == to_low)
    helped = (ctx == half) | (ctx == half - 1)
    helper_pair = {"ctx": jnp.where(ctx == from_low, half, jnp.where(ctx == half, from_low, jnp.where(ctx == to_low, half - 1, to_low)))}
    aside = 1 - 2 * lax.div(x, 2)

    def turn_z(amount):
        return wrap(wrap(z + amount + NZ, NZ), NZ)

    def sum_y_peer(t, amount):
        its_yl = (t // 2) % 2
        return its_yl, {
            "dp": (t // 4) * 2 + t % 2,
            "ctx": ctx + (its_yl - yl) * half + (turn_z(amount) - z) * NX,
        }

    def sum_x_peer(t, amount):
        return {"ctx": ctx + t - x + (turn_z(amount) - z) * NX}

    def load(which, i):
        src, dst = ((k_h, k), (v_h, v), (q_h, q), (go_h, go))[which]
        at = pl.ds(pl.multiple_of(i * lrows, lrows), lrows)
        return pltpu.make_async_copy(src.at[at], dst.at[at], load_sem.at[which, i])

    barrier = pltpu.get_barrier_semaphore()
    middle = (x == 1) | (x == 2)
    greeted = [sum_y_peer(t, -aside)[1] for t in range(NY)] + [right, left]
    greeted += [x_peer(d)[1] for d in range(1, NX)]
    greeted += [z_peer(d)[1] for d in range(1, NZ)]
    greeted += [sum_x_peer(t, 2 * (t // 2) - 1) for t in range(NX)]
    for device in greeted:
        pl.semaphore_signal(barrier, inc=1, device_id=device, device_id_type=MESH)

    @pl.when(jnp.logical_not(middle))
    def _():
        for d in range(1, NZ):
            pl.semaphore_signal(barrier, inc=1, device_id=beside_peer(d), device_id_type=MESH)

    @pl.when(jnp.logical_not(helped))
    def _():
        pl.semaphore_signal(barrier, inc=1, device_id=other_half, device_id_type=MESH)

    @pl.when(helped)
    def _():
        pl.semaphore_signal(barrier, inc=1, device_id=helper_pair, device_id_type=MESH)

    taps_load = pltpu.make_async_copy(f_h, xg.at[x], const_sem.at[0])
    taps_load.start()
    for i in range(LOADS):
        load(0, i).start()
        load(1, i).start()
        load(2, LOADS - 1 - i).start()
        load(3, LOADS - 1 - i).start()
    consts = [
        pltpu.make_async_copy(src, dst, const_sem.at[1 + n])
        for n, (src, dst) in enumerate(((into_h, into), (back_h, back), (tap_h, tap)))
    ]
    for c in consts:
        c.start()

    def at_step(i):
        return pl.ds(pl.multiple_of(i * srows, srows), srows)

    def send_p(i):
        return pltpu.make_async_remote_copy(
            src_ref=p.at[at_step(i)], dst_ref=prev.at[at_step(i)],
            send_sem=hs.at[0, i], recv_sem=hr.at[0, i],
            device_id=right, device_id_type=MESH,
        )

    def send_gf(i):
        return pltpu.make_async_remote_copy(
            src_ref=gf.at[at_step(i)], dst_ref=nxt.at[at_step(i)],
            send_sem=hs.at[1, i], recv_sem=hr.at[1, i],
            device_id=left, device_id_type=MESH,
        )

    def products(i):
        j = LOADS - 1 - i
        load(0, i).wait()
        load(1, i).wait()
        at = pl.ds(pl.multiple_of(i * lrows, lrows), lrows)
        p[at, :] = (k[at, :].astype(F32) * v[at, :].astype(F32)).astype(BF16)
        load(2, j).wait()
        load(3, j).wait()
        at = pl.ds(pl.multiple_of(j * lrows, lrows), lrows)
        gf[at, :] = (q[at, :].astype(F32) * go[at, :].astype(F32)).astype(BF16)

    products(0)
    taps_load.wait()
    count = len(greeted) + jnp.where(middle, NZ - 1, 0) + jnp.where(unable, 0, 1) + jnp.where(helper, 1, 0)
    pl.semaphore_wait(barrier, count)

    gather_x = [
        pltpu.make_async_remote_copy(
            src_ref=xg.at[x], dst_ref=xg.at[x],
            send_sem=xs.at[d - 1], recv_sem=xr.at[d - 1],
            device_id=x_peer(d)[1], device_id_type=MESH,
        )
        for d in range(1, NX)
    ]
    gather_z = [
        [
            pltpu.make_async_remote_copy(
                src_ref=zg.at[yl, z], dst_ref=zg.at[yl, z],
                send_sem=zs.at[n, d - 1], recv_sem=zr.at[d - 1],
                device_id=device, device_id_type=MESH,
            )
            for n, device in enumerate((z_peer(d)[1], beside_peer(d)))
        ]
        for d in range(1, NZ)
    ]
    gather_y, gather_help = (
        pltpu.make_async_remote_copy(
            src_ref=zg.at[yl], dst_ref=zg.at[yl], send_sem=ys.at[n], recv_sem=yr,
            device_id=device, device_id_type=MESH,
        )
        for n, device in enumerate((other_half, helper_pair))
    )
    reduce_z, reduce_y, reduce_x = [], [], []
    for d in range(1, NZ):
        other, device = z_peer(d)
        reduce_z.append(
            pltpu.make_async_remote_copy(
                src_ref=sa.at[wrap(other + 2 * aside + jnp.where(aside < 0, NZ, 0), NZ)], dst_ref=ra.at[z],
                send_sem=as_.at[d - 1], recv_sem=ar.at[d - 1],
                device_id=device, device_id_type=MESH,
            )
        )
    for t in range(NY):
        its_yl, device = sum_y_peer(t, aside)
        reduce_y.append(
            pltpu.make_async_remote_copy(
                src_ref=sb.at[its_yl], dst_ref=rb.at[y],
                send_sem=bs.at[t], recv_sem=br.at[y],
                device_id=device, device_id_type=MESH,
            )
        )
    for t in range(NX):
        reduce_x.append(
            pltpu.make_async_remote_copy(
                src_ref=sc.at[t], dst_ref=rc.at[x],
                send_sem=cs.at[t], recv_sem=cr.at[x],
                device_id=sum_x_peer(t, aside), device_id_type=MESH,
            )
        )

    def wait_sum(copies, landed, recv_sems):
        for n, c in enumerate(copies):
            c.wait_send()
            pltpu.make_async_remote_copy(
                src_ref=landed.at[n], dst_ref=landed.at[n],
                send_sem=recv_sems.at[n], recv_sem=recv_sems.at[n],
                device_id=right, device_id_type=MESH,
            ).wait_recv()

    for c in gather_x:
        c.start()

    paced_p, paced_gf = (x == NX - 1) & (ctx < last), (x == 0) & (ctx > 0)

    def send(n):
        @pl.when(paced_p)
        def _():
            send_p(n).start()

        @pl.when(paced_gf)
        def _():
            send_gf(STEPS - 1 - n).start()

    def send_first(i):
        for n in range(per_load):
            n = i * per_load + n

            @pl.when((ctx < last) & ((x < NX - 1) | (n < AHEAD)))
            def _():
                send_p(n).start()

            @pl.when((ctx > 0) & ((x > 0) | (n < AHEAD)))
            def _():
                send_gf(STEPS - 1 - n).start()

    send_first(0)

    @pl.loop(1, LOADS)
    def _(i):
        products(i)
        send_first(i)

    @pl.when(ctx == 0)
    def _():
        prev[...] = jnp.zeros_like(prev)

    @pl.when(ctx == last)
    def _():
        nxt[...] = jnp.zeros_like(nxt)

    for c in consts:
        c.wait()
    for c in gather_x:
        c.wait()
    mine = jnp.concatenate([xg[i] for i in range(NX)], axis=0)
    zg[yl, z] = jnp.concatenate([mine[:, :TAPS], mine[:, TAPS:]], axis=0).astype(BF16)

    @pl.when(middle)
    def _():
        for pair in gather_z:
            for c in pair:
                c.start()

    def spread(a):
        return jnp.broadcast_to(a[:, None, :], (groups, MEMBERS, TAPS)).reshape(srows, TAPS)

    def group_rows(i):
        return pl.ds(pl.multiple_of(i * groups, groups), groups)

    def positions(re, im, which):
        high, low = two_parts(jnp.concatenate([re, im], axis=1))
        both = dot(high, back[which])
        return both[:, :TAPS] + both[:, TAPS:] + dot(low, back[which, :, :TAPS])

    def arrived(i):
        @pl.when(ctx > 0)
        def _():
            send_p(i).wait_recv()

        @pl.when(ctx < last)
        def _():
            send_gf(STEPS - 1 - i).wait_recv()

    def forward_window(i):
        before, own = prev[at_step(i), :], p[at_step(i), :]
        return dot(jnp.concatenate([before, before, own, own], axis=1), into[...])

    def backward_window(i):
        own, after = gf[at_step(i), :], nxt[at_step(i), :]
        return dot(jnp.concatenate([own, own, after, after], axis=1), into[...])

    def forward_outputs(i, window):
        at = at_step(i)
        re, im = window[:, :TAPS], window[:, TAPS:]
        hre, him = spread(spec[group_rows(i), :TAPS]), spread(spec[group_rows(i), TAPS:])
        filtered = positions(re * hre - im * him, re * him + im * hre, 0)
        mixed[at, :] = (q[at, :].astype(F32) * filtered).astype(BF16)
        gq[at, :] = (go[at, :].astype(F32) * filtered).astype(BF16)

    def backward_outputs(i, window):
        at = at_step(i)
        re, im = window[:, :TAPS], window[:, TAPS:]
        hre, him = spread(spec[group_rows(i), :TAPS]), spread(spec[group_rows(i), TAPS:])
        grad = positions(re * hre + im * him, im * hre - re * him, 1)
        gk[at, :] = (v[at, :].astype(F32) * grad).astype(BF16)
        gv[at, :] = (k[at, :].astype(F32) * grad).astype(BF16)

    def tap_products(i, g, b):
        def total(a):
            return jnp.sum(a.reshape(groups, MEMBERS, TAPS), axis=1)

        gre, gim, bre, bim = g[:, :TAPS], g[:, TAPS:], b[:, :TAPS], b[:, TAPS:]
        dspec[group_rows(i), :TAPS] = total(gre * bre + gim * bim)
        dspec[group_rows(i), TAPS:] = total(gim * bre - gre * bim)

    @pl.loop(0, STEPS // 2)
    def _(i):
        @pl.when(i + AHEAD < STEPS // 2 + LATER)
        def _():
            send(i + AHEAD)

        arrived(i)
        j = STEPS - 1 - i
        fw, bw = forward_window(i), backward_window(j)
        g, b = gf[at_step(i), :], p[at_step(j), :]
        gw = dot(jnp.concatenate([g, g], axis=1), into[WINDOW:, :])
        bp = dot(jnp.concatenate([b, b], axis=1), into[:WINDOW, :])
        tap_products(i, gw, fw)
        tap_products(j, bw, bp)
        fspec[at_step(i), :] = fw
        bspec[at_step(i), :] = bw

        @pl.when(i == 2)
        def _():
            for pair in gather_z:
                pair[0].wait_recv()

            @pl.when(jnp.logical_not(unable))
            def _():
                gather_y.start()

            @pl.when(helper)
            def _():
                gather_help.start()

    high, low = two_parts(dspec[...])
    grads = lax.dot_general(
        tap[...], jnp.concatenate([high, high, low], axis=1),
        (((1,), (1,)), ((), ())), preferred_element_type=F32,
    )
    sa[...] = grads.astype(BF16).reshape(sa.shape)
    ra[z] = sa[turn_z(2 * aside)]
    for c in reduce_z:
        c.start()
    for n in range(LATER, DEEP):
        send(STEPS // 2 + n)

    gather_y.wait_recv()

    @pl.when(jnp.logical_not(unable))
    def _():
        gather_y.wait_send()

    @pl.when(helper)
    def _():
        gather_help.wait_send()

    @pl.when(middle)
    def _():
        for pair in gather_z:
            for c in pair:
                c.wait_send()

    tiles = [zg[a, b].astype(F32) for a in range(NYL) for b in range(NZ)]
    taps = jnp.concatenate([jnp.concatenate([t[:8], t[8:]], axis=1) for t in tiles], axis=0).T.astype(BF16)
    spec[...] = dot(jnp.concatenate([taps, taps], axis=1), into[:WINDOW, :])

    @pl.loop(STEPS // 2, STEPS)
    def _(i):
        @pl.when(i + DEEP < STEPS)
        def _():
            send(i + DEEP)

        old = i - STEPS // 2
        forward_outputs(old, fspec[at_step(old), :])
        backward_outputs(STEPS - 1 - old, bspec[at_step(old), :])
        arrived(i)
        forward_outputs(i, forward_window(i))
        backward_outputs(STEPS - 1 - i, backward_window(STEPS - 1 - i))

        @pl.when(i == STEPS // 2 + 1)
        def _():
            for c in reduce_z:
                c.wait()
            sb[...] = jnp.sum(ra[...].astype(F32), axis=0).reshape(sb.shape)
            for c in reduce_y:
                c.start()

        @pl.when(i == STEPS // 2 + 4)
        def _():
            wait_sum(reduce_y, rb, br)
            part = jnp.sum(rb[...], axis=0)
            for n in range(NX):
                sc[n] = part[2 * n : 2 * n + 2]
            for c in reduce_x:
                c.start()

    wait_sum(reduce_x, rc, cr)
    gfilt[...] = jnp.sum(rc[...], axis=0)

    @pl.loop(0, STEPS)
    def _(i):
        @pl.when(ctx < last)
        def _():
            send_p(i).wait_send()

        @pl.when(ctx > 0)
        def _():
            send_gf(i).wait_send()


def write_kernel(*refs):
    count = len(refs) // 2
    sems = refs[-1]
    copies = [
        pltpu.make_async_copy(refs[i], refs[count + i], sems.at[i]) for i in range(count)
    ]
    for c in copies:
        c.start()
    for c in copies:
        c.wait()


def local(queries, keys_in, values_in, filters, grad_out):
    rows, width = queries.shape[1:]
    groups = filters.shape[0]
    into, back, tap = (jnp.asarray(m) for m in transforms())
    slab = (rows, width)
    dma = pltpu.SemaphoreType.DMA
    anywhere = pl.BlockSpec(memory_space=pl.ANY)
    in_vmem = pl.BlockSpec(memory_space=pltpu.VMEM)
    operands = [queries[0], keys_in[0], values_in[0], grad_out[0], filters.T, into, back, tap]
    operands = [pltpu.with_memory_space_constraint(a, pltpu.HBM) for a in operands]
    outs = pl.pallas_call(
        mixer_kernel,
        out_shape=[pltpu.VMEM(slab, BF16)] * 4 + [pltpu.VMEM((2, groups), F32)],
        in_specs=[anywhere] * len(operands),
        out_specs=[in_vmem] * 5,
        scratch_shapes=[
            *[pltpu.VMEM(slab, BF16)] * 8,
            pltpu.VMEM(into.shape, BF16), pltpu.VMEM(back.shape, BF16), pltpu.VMEM(tap.shape, BF16),
            pltpu.VMEM((NX, 2, groups), F32), pltpu.VMEM((NYL, NZ, 16, TAPS), BF16),
            pltpu.VMEM((groups, WINDOW), F32), pltpu.VMEM((groups, WINDOW), F32),
            pltpu.VMEM((rows // 2, WINDOW), F32), pltpu.VMEM((rows // 2, WINDOW), F32),
            pltpu.VMEM((NZ, 16, groups), BF16), pltpu.VMEM((NZ, 16, groups), BF16),
            pltpu.VMEM((NYL, 8, groups), F32), pltpu.VMEM((NY, 8, groups), F32),
            pltpu.VMEM((NX, 2, groups), F32), pltpu.VMEM((NX, 2, groups), F32),
            dma((4, LOADS)), dma((4,)), dma((2, STEPS)), dma((2, STEPS)),
            dma((NX - 1,)), dma((NX - 1,)), dma((2, NZ - 1)), dma((NZ - 1,)), dma((2,)), dma,
            dma((NZ - 1,)), dma((NZ - 1,)), dma((NY,)), dma((NY,)),
            dma((NX,)), dma((NX,)),
        ],
        compiler_params=pltpu.CompilerParams(
            collective_id=0, has_side_effects=True, vmem_limit_bytes=40 * 2**20
        ),
        name="mixer",
    )(*operands)
    outs = [pltpu.with_memory_space_constraint(a, pltpu.VMEM) for a in outs]
    written = pl.pallas_call(
        write_kernel,
        out_shape=[pltpu.HBM(a.shape, a.dtype) for a in outs],
        in_specs=[anywhere] * 5,
        out_specs=[anywhere] * 5,
        scratch_shapes=[dma((5,))],
        compiler_params=pltpu.CompilerParams(vmem_limit_bytes=2**20),
        name="write",
    )(*outs)
    return (*[a[None] for a in written[:4]], written[4].T)


def solution(mesh):
    return jax.shard_map(
        local,
        mesh=mesh,
        in_specs=(
            P("dp", None, "ctx"),
            P("dp", None, "ctx"),
            P("dp", None, "ctx"),
            P(None, "ctx"),
            P("dp", None, "ctx"),
        ),
        out_specs=(
            P("dp", None, "ctx"),
            P("dp", None, "ctx"),
            P("dp", None, "ctx"),
            P("dp", None, "ctx"),
            P(None, "ctx"),
        ),
        check_vma=False,
    )
```
